32 devices in a mesh: row: 16 (over z, y, core), col: 2 (over x).
Axes of the slice: x: 2, y: 2, z: 4, core: 2. Of those that a mesh axis runs over, the one named last changes fastest.
Arguments:
- left: float32 [128, 8192], P('col', 'row'), may hold values from -12 to 12
- right: float32 [128, 8192], P('row', 'col'), may hold values from -12 to 12
- w_out: float32 [1024, 128], replicated, may hold values from -0.1875 to 0.1875
- b_out: float32 [128], replicated, may hold values from -3 to 3
- pair_grad: float32 [256, 256, 128], P('row', 'col'), may hold values from -6 to 6
Outputs:
- pair_out: float32 [256, 256, 128], P('row', 'col')
- grad_left: float32 [128, 8192], P('col', 'row')
- grad_right: float32 [128, 8192], P('row', 'col')
- grad_weight: float32 [1024, 128], replicated
- grad_bias: float32 [128], replicated
The draws below stay inside these ranges and needn't reach their ends.
All inputs are finite; a program needn't handle non-finite values.
Results may differ from the reference program's by a relative error of at most 0.0001.
Values sent between devices are 32-bit elements; how exact they have to be, the bound alone decides.
A program may use at most 128 MiB of HBM per device.

```python
import jax
import jax.numpy as jnp
from jax import lax

C = 32
Z = 128
S = 128
R = 256
N_ROW = 16


def shard_levels(rng, dims, cuts, least, top_value):
    loudness = 1.0
    for position, blocks in cuts:
        draws = jax.random.uniform(jax.random.fold_in(jax.random.fold_in(rng, 6), position), (blocks,), jnp.float32, least / len(cuts), top_value / len(cuts))
        loudness = loudness * jnp.repeat(jnp.exp(draws), dims[position] // blocks).reshape((-1,) + (1,) * (len(dims) - 1 - position))
    return loudness


def normal_values(key, extent, deviation, reach, pieces=(), held_as=jnp.bfloat16):
    values = deviation * jax.random.normal(key, extent, jnp.float32)
    if pieces:
        values = values * shard_levels(key, extent, pieces, -0.22, 0.18)
    return jnp.clip(values, -reach, reach).astype(held_as)


def setup_inputs(seed: int = 0) -> dict:
    streams_of = jax.random.split(jax.random.key(seed), 6)
    return {
        "left": normal_values(streams_of[0], (S, R * C), 2.0, 12.0, ((0, 2), (1, 16)), jnp.float32),
        "right": normal_values(streams_of[1], (S, R * C), 2.0, 12.0, ((0, 16), (1, 2)), jnp.float32),
        "w_out": normal_values(streams_of[2], (C * C, Z), (C * C) ** -0.5, 0.1875, (), jnp.float32),
        "b_out": normal_values(streams_of[3], (Z,), 0.5, 3.0, (), jnp.float32),
        "pair_grad": normal_values(streams_of[4], (R, R, Z), 1.0, 6.0, ((0, 16), (1, 2)), jnp.float32),
    }


def reference(left, right, w_out, b_out, pair_grad):
    highest = lax.Precision.HIGHEST
    block_rows = R // N_ROW
    weight_cube = w_out.reshape(C, C, Z)

    def advance(carry, block_index):
        sum_right, sum_weight, sum_bias = carry
        left_block = lax.dynamic_slice_in_dim(left, block_index * (block_rows * C), block_rows * C, 1)
        outer = lax.dot_general(left_block, right, (((0,), (0,)), ((), ())), precision=highest,
                                preferred_element_type=jnp.float32) / S
        outer_split = outer.reshape(block_rows, C, R, C)
        grad_tile = lax.dynamic_slice_in_dim(pair_grad, block_index * block_rows, block_rows, 0)
        out_block = jnp.einsum("icje,cez->ijz", outer_split, weight_cube, precision=highest) + b_out
        grad_outer = jnp.einsum("ijz,cez->icje", grad_tile, weight_cube, precision=highest)
        grad_outer = grad_outer.reshape(block_rows * C, R * C)
        left_block_grad = lax.dot_general(right, grad_outer, (((1,), (1,)), ((), ())), precision=highest,
                                          preferred_element_type=jnp.float32) / S
        right_term = jnp.dot(left_block, grad_outer, precision=highest) / S
        weight_term = jnp.einsum("icje,ijz->cez", outer_split, grad_tile, precision=highest)
        carry = (sum_right + right_term, sum_weight + weight_term, sum_bias + jnp.sum(grad_tile, axis=(0, 1)))
        return carry, (out_block, left_block_grad)

    start_carry = (jnp.zeros((S, R * C), jnp.float32), jnp.zeros((C, C, Z), jnp.float32),
                   jnp.zeros((Z,), jnp.float32))
    (grad_right, sum_weight, sum_bias), (outs, lefts) = lax.scan(
        advance, start_carry, jnp.arange(N_ROW, dtype=jnp.int32))
    pair_out = outs.reshape(R, R, Z)
    grad_left = jnp.transpose(lefts, (1, 0, 2)).reshape(S, R * C)
    grad_weight = sum_weight.reshape(C * C, Z) / R
    grad_bias = sum_bias / R
    return (pair_out, grad_left, grad_right, grad_weight, grad_bias)
```

```python
import functools

import jax
import jax.numpy as jnp
from jax import lax
from jax.experimental import pallas as pl
from jax.experimental.pallas import tpu as pltpu
from jax.sharding import PartitionSpec as P

C = 32
Z = 128
S = 128
LANES = 128
BF = jnp.bfloat16
F32 = jnp.float32
NN = (((1,), (0,)), ((), ()))
NT = (((1,), (1,)), ((), ()))


def split(x):
    high = x.astype(BF)
    return high, (x - high.astype(F32)).astype(BF)


def mm(a, b, dims):
    return lax.dot_general(a, b, dims, preferred_element_type=F32)


def split_grad(pg, pgh, pgl, gb):
    rows = pg.shape[0]
    step = min(rows, 512)

    def one(k, total):
        at = pl.ds(pl.multiple_of(k * step, step), step)
        x = pg[at, :]
        high, low = split(x)
        pgh[at, :] = high
        pgl[at, :] = low
        return total + jnp.sum(x.reshape(step // 8, 8, x.shape[1]), axis=0)

    total = lax.fori_loop(0, rows // step, one, jnp.zeros((8, pg.shape[1]), F32))
    gb[...] = jnp.sum(total, axis=0, keepdims=True)


def make_grad_outer(pgh, pgl, w, gh, gl, tj):
    wh, wl = split(w[...])
    both = jnp.concatenate([wh, wl], axis=1)
    group = 2

    def one(k, carry):
        at = pl.ds(pl.multiple_of(k * group * tj, group * tj), group * tj)
        ph, low = pgh[at, :], pgl[at, :]
        g = mm(both, jnp.concatenate([ph, ph], axis=1), NT) + mm(wh, low, NT)
        high, low = split(g)
        for i in range(group):
            rows = pl.ds(pl.multiple_of(k * group * C + i * C, C), C)
            for e in range(C):
                gh[rows, e * tj : (e + 1) * tj] = high[e * C : (e + 1) * C, i * tj : (i + 1) * tj]
                gl[rows, e * tj : (e + 1) * tj] = low[e * C : (e + 1) * C, i * tj : (i + 1) * tj]
        return carry

    lax.fori_loop(0, pgh.shape[0] // (group * tj), one, 0)


def make_grad_right(a, gh, gl, put, width):
    ah, al = split(a[...])
    both = jnp.concatenate([ah, al], axis=0)

    def one(k, carry):
        cols = pl.ds(pl.multiple_of(k * width, width), width)
        high, low = gh[:, cols], gl[:, cols]
        r = mm(both, high, NN)
        r = r[:S] + r[S:] + mm(ah, low, NN)
        put(cols, r * (1.0 / S))
        return carry

    lax.fori_loop(0, gh.shape[1] // width, one, 0)


def make_outer(a, bh, bl, oh, ol, tj):
    ath, atl = split(a[...].T * (1.0 / S))
    both = jnp.concatenate([ath, atl], axis=1)
    ti = a.shape[1] // C
    group = 4
    width = group * tj

    def one(k, carry):
        cols = pl.ds(pl.multiple_of(k * width, width), width)
        high, low = bh[:, cols], bl[:, cols]
        o = mm(both, jnp.concatenate([high, high], axis=0), NN) + mm(ath, low, NN)
        high, low = split(o)
        for e in range(group):
            rows = pl.ds(pl.multiple_of(k * group * C + e * C, C), C)
            for i in range(ti):
                oh[rows, i * tj : (i + 1) * tj] = high[i * C : (i + 1) * C, e * tj : (e + 1) * tj]
                ol[rows, i * tj : (i + 1) * tj] = low[i * C : (i + 1) * C, e * tj : (e + 1) * tj]
        return carry

    lax.fori_loop(0, bh.shape[1] // width, one, 0)


def make_grad_weight(oh, ol, pgh, pgl, gw, scale):
    step = 256

    def one(k, carry):
        rows = pl.ds(pl.multiple_of(k * step, step), step)
        ph = pgh[...]
        r = mm(oh[rows, :], jnp.concatenate([ph, pgl[...]], axis=1), NN)
        gw[rows, :] = (r[:, :Z] + r[:, Z:] + mm(ol[rows, :], ph, NN)) * scale
        return carry

    lax.fori_loop(0, oh.shape[0] // step, one, 0)


def make_pair_out(oh, ol, w, bias, out, width):
    wh, wl = split(w[...].T)
    both = jnp.concatenate([wh, wl], axis=0)

    def one(k, carry):
        cols = pl.ds(pl.multiple_of(k * width, width), width)
        r = mm(both, oh[:, cols], NN)
        r = r[:Z] + r[Z:] + mm(wh, ol[:, cols], NN)
        out[cols, :] = r.T + bias[...]
        return carry

    lax.fori_loop(0, oh.shape[1] // width, one, 0)


def make_grad_left(bh, bl, gh, gl, put, step):
    both = jnp.concatenate([bh[...], bl[...]], axis=0)
    for k in range(gh.shape[0] // step):
        rows = slice(k * step, (k + 1) * step)
        r = mm(both, gh[rows, :], NT)
        r = r[:S] + r[S:] + mm(bh[...], gl[rows, :], NT)
        put(rows, r * (1.0 / S))


def first_kernel(tj, a, pg, w, gr, gh, gl, pgh, pgl, gb):
    split_grad(pg, pgh, pgl, gb)
    make_grad_outer(pgh, pgl, w, gh, gl, tj)

    def put(cols, r):
        gr[:, cols] = r

    make_grad_right(a, gh, gl, put, 4 * tj)


def second_kernel(tj, scale, a, b, w, bias, gh, gl, pgh, pgl, out, left, gw, bh, bl, oh, ol):
    high, low = split(b[...])
    bh[...] = high
    bl[...] = low
    make_outer(a, bh, bl, oh, ol, tj)
    make_grad_weight(oh, ol, pgh, pgl, gw, scale)

    def put(cols, r):
        left[:, cols] = r

    make_grad_left(bh, bl, gh, gl, put, 256)
    make_pair_out(oh, ol, w, bias, out, 2 * tj)


def fast(left, right, w_out, b_out, pair_grad):
    ti = left.shape[1] // C
    tj = right.shape[1] // C
    pairs = ti * tj
    residues = ti * lax.axis_size("row")
    scale = 1.0 / residues
    vmem = pl.BlockSpec(memory_space=pltpu.VMEM)
    params = pltpu.CompilerParams(vmem_limit_bytes=56 * 1024 * 1024)
    w = w_out.reshape(C, C, Z).transpose(1, 0, 2).reshape(C * C, Z)
    pg = pair_grad.reshape(pairs, Z)
    mine = right.reshape(-1, tj, C).transpose(0, 2, 1).reshape(right.shape)
    a = lax.all_gather(left, "col", axis=0, tiled=True)
    b = lax.all_gather(mine, "row", axis=0, tiled=True)
    flops = 2 * pairs * C * C * Z * 3
    shape = jax.ShapeDtypeStruct
    gr, gh, gl, pgh, pgl, gb = pl.pallas_call(
        functools.partial(first_kernel, tj),
        out_shape=[
            shape((S, C * tj), F32),
            shape((ti * C, C * tj), BF),
            shape((ti * C, C * tj), BF),
            shape((pairs, Z), BF),
            shape((pairs, Z), BF),
            shape((1, Z), F32),
        ],
        in_specs=[vmem] * 3,
        out_specs=[vmem] * 6,
        compiler_params=params,
        cost_estimate=pl.CostEstimate(flops=2 * flops, bytes_accessed=1 << 24, transcendentals=0),
        name="grads_of_outer",
    )(a, pg, w)
    grad_right = lax.psum_scatter(gr, "row", scatter_dimension=0, tiled=True)
    out, part, gw = pl.pallas_call(
        functools.partial(second_kernel, tj, scale),
        out_shape=[
            shape((pairs, Z), F32),
            shape((S, ti * C), F32),
            shape((C * C, Z), F32),
        ],
        in_specs=[vmem] * 8,
        out_specs=[vmem] * 3,
        scratch_shapes=[
            pltpu.VMEM((S, C * tj), BF),
            pltpu.VMEM((S, C * tj), BF),
            pltpu.VMEM((C * C, pairs), BF),
            pltpu.VMEM((C * C, pairs), BF),
        ],
        compiler_params=params,
        cost_estimate=pl.CostEstimate(flops=4 * flops, bytes_accessed=1 << 24, transcendentals=0),
        name="outer_and_rest",
    )(a, b, w, b_out.reshape(1, Z), gh, gl, pgh, pgl)
    grad_left = lax.psum_scatter(part, "col", scatter_dimension=0, tiled=True)
    gb8 = jnp.broadcast_to(gb * (scale / 8), (8, Z))
    total = lax.psum(jnp.concatenate([gw, gb8], axis=0), ("row", "col"))
    grad_weight = total[: C * C].reshape(C, C, Z).transpose(1, 0, 2).reshape(C * C, Z)
    grad_bias = jnp.sum(total[C * C :], axis=0)
    grad_right = grad_right.reshape(-1, C, tj).transpose(0, 2, 1).reshape(right.shape)
    return (out.reshape(pair_grad.shape), grad_left, grad_right, grad_weight, grad_bias)


def plain(left, right, w_out, b_out, pair_grad):
    high = lax.Precision.HIGHEST
    ti = left.shape[1] // C
    tj = right.shape[1] // C
    residues = ti * lax.axis_size("row")
    cube = w_out.reshape(C, C, Z)
    a = lax.all_gather(left, "col", axis=0, tiled=True)
    b = lax.all_gather(right, "row", axis=0, tiled=True)
    outer = lax.dot_general(a, b, (((0,), (0,)), ((), ())), precision=high) / S
    cut = outer.reshape(ti, C, tj, C)
    pair_out = jnp.einsum("icje,cez->ijz", cut, cube, precision=high) + b_out
    g = jnp.einsum("ijz,cez->icje", pair_grad, cube, precision=high)
    g = g.reshape(ti * C, tj * C)
    part = lax.dot_general(b, g, NT, precision=high) / S
    grad_left = lax.psum_scatter(part, "col", scatter_dimension=0, tiled=True)
    part = jnp.dot(a, g, precision=high) / S
    grad_right = lax.psum_scatter(part, "row", scatter_dimension=0, tiled=True)
    gw = jnp.einsum("icje,ijz->cez", cut, pair_grad, precision=high).reshape(C * C, Z)
    gw, gb = lax.psum((gw, jnp.sum(pair_grad, axis=(0, 1))), ("row", "col"))
    return (pair_out, grad_left, grad_right, gw / residues, gb / residues)


def body(left, right, w_out, b_out, pair_grad):
    tiles_fit = (right.shape[1] // C) % LANES == 0 and (left.shape[1] // C) % 4 == 0
    return (fast if tiles_fit else plain)(left, right, w_out, b_out, pair_grad)


def solution(mesh):
    placed = (P("col", "row"), P("row", "col"), P(), P(), P("row", "col", None))
    return jax.shard_map(
        body,
        mesh=mesh,
        in_specs=placed,
        out_specs=(P("row", "col", None), P("col", "row"), P("row", "col"), P(), P()),
        check_vma=False,
    )
```

```python
import functools

import jax
import jax.numpy as jnp
from jax import lax
from jax.experimental import pallas as pl
from jax.experimental.pallas import tpu as pltpu
from jax.sharding import PartitionSpec as P

C = 32
Z = 128
S = 128
LANES = 128
BF = jnp.bfloat16
F32 = jnp.float32
NN = (((1,), (0,)), ((), ()))
NT = (((1,), (1,)), ((), ()))


def split(x):
    high = x.astype(BF)
    return high, (x - high.astype(F32)).astype(BF)


def mm(a, b, dims):
    return lax.dot_general(a, b, dims, preferred_element_type=F32)


def bit_reverse(value, bits):
    return sum(((value >> k) & 1) << (bits - 1 - k) for k in range(bits))


def split_grad(pg, pgh, pgl):
    rows = pg.shape[0]
    step = min(rows, 512)

    def one(k, total):
        at = pl.ds(pl.multiple_of(k * step, step), step)
        x = pg[at, :]
        high, low = split(x)
        pgh[at, :] = high
        pgl[at, :] = low
        return total + jnp.sum(x.reshape(step // 8, 8, x.shape[1]), axis=0)

    return lax.fori_loop(0, rows // step, one, jnp.zeros((8, pg.shape[1]), F32))


def make_grad_outer(pgh, pgl, w, gh, gl, tj, first, last):
    wh, wl = split(w[...])
    both = jnp.concatenate([wh, wl], axis=1)
    group = 2

    def one(k, carry):
        at = pl.ds(pl.multiple_of(k * group * tj, group * tj), group * tj)
        ph, low = pgh[at, :], pgl[at, :]
        g = mm(both, jnp.concatenate([ph, ph], axis=1), NT) + mm(wh, low, NT)
        high, low = split(g)
        for i in range(group):
            rows = pl.ds(pl.multiple_of(k * group * C + i * C, C), C)
            for e in range(C):
                gh[rows, e * tj : (e + 1) * tj] = high[e * C : (e + 1) * C, i * tj : (i + 1) * tj]
                gl[rows, e * tj : (e + 1) * tj] = low[e * C : (e + 1) * C, i * tj : (i + 1) * tj]
        return carry

    lax.fori_loop(first, last, one, 0)


def make_grad_right(a, gh, gl, acc, width):
    n, rows, _ = acc.shape
    bits = n.bit_length() - 1
    ah, al = split(a * (1.0 / S))
    both = jnp.concatenate([ah, al], axis=0)

    def one(k, carry):
        cols = pl.ds(pl.multiple_of(k * width, width), width)
        high, low = gh[:, cols], gl[:, cols]
        r = mm(both, high, NN)
        r = r[:S] + r[S:] + mm(ah, low, NN)
        for p in range(n):
            acc[bit_reverse(p, bits), :, cols] = r[p * rows : (p + 1) * rows]
        return carry

    lax.fori_loop(0, gh.shape[1] // width, one, 0)


def split_right(raw, bh, bl, width):
    n = raw.shape[0]
    bits = n.bit_length() - 1

    def one(k, carry):
        cols = pl.ds(pl.multiple_of(k * width, width), width)
        x = jnp.concatenate([raw[bit_reverse(p, bits), :, cols] for p in range(n)], axis=0)
        high, low = split(x)
        bh[:, cols] = high
        bl[:, cols] = low
        return carry

    lax.fori_loop(0, bh.shape[1] // width, one, 0)


def make_outer(a, bh, bl, oh, ol, tj):
    ath, atl = split(a.T * (1.0 / S))
    both = jnp.concatenate([ath, atl], axis=1)
    ti = a.shape[1] // C
    group = 4
    width = group * tj

    def one(k, carry):
        cols = pl.ds(pl.multiple_of(k * width, width), width)
        high, low = bh[:, cols], bl[:, cols]
        o = mm(both, jnp.concatenate([high, high], axis=0), NN) + mm(ath, low, NN)
        high, low = split(o)
        for e in range(group):
            rows = pl.ds(pl.multiple_of(k * group * C + e * C, C), C)
            for i in range(ti):
                oh[rows, i * tj : (i + 1) * tj] = high[i * C : (i + 1) * C, e * tj : (e + 1) * tj]
                ol[rows, i * tj : (i + 1) * tj] = low[i * C : (i + 1) * C, e * tj : (e + 1) * tj]
        return carry

    lax.fori_loop(0, bh.shape[1] // width, one, 0)


def make_grad_weight(oh, ol, pgh, pgl, acc, column_sums, scale):
    slots, held, _ = acc.shape
    piece = held - 8
    group = 256 // piece
    step = group * piece

    def one(k, carry):
        rows = pl.ds(pl.multiple_of(k * step, step), step)
        ph = pgh[...]
        r = mm(oh[rows, :], jnp.concatenate([ph, pgl[...]], axis=1), NN)
        r = (r[:, :Z] + r[:, Z:] + mm(ol[rows, :], ph, NN)) * scale
        for g in range(group):
            acc[k * group + g, :piece, :] = r[g * piece : (g + 1) * piece]
            acc[k * group + g, piece:, :] = column_sums * scale
        return carry

    lax.fori_loop(0, slots // group, one, 0)


def make_pair_out(oh, ol, w, bias, out, width, first, last):
    wh, wl = split(w[...].T)
    both = jnp.concatenate([wh, wl], axis=0)

    def one(k, carry):
        cols = pl.ds(pl.multiple_of(k * width, width), width)
        r = mm(both, oh[:, cols], NN)
        r = r[:Z] + r[Z:] + mm(wh, ol[:, cols], NN)
        out[cols, :] = r.T + bias[...]
        return carry

    lax.fori_loop(first, last, one, 0)


def make_grad_left(bh, bl, gh, gl, part, first, last):
    both = jnp.concatenate([bh[...], bl[...]], axis=0)
    r = mm(both, gh[first:last, :], NT)
    r = (r[:S] + r[S:] + mm(bh[...], gl[first:last, :], NT)) * (1.0 / S)
    half = part.shape[1]
    for h in range(2):
        part[h, :, first:last] = r[h * half : (h + 1) * half]


def kernel(
    n, tj, scale, left, mine, pg, w, bias, out, grad_left, grad_right, grad_weight, grad_bias,
    a_raw, b_raw, r_acc, r_in, l_part, l_in, w_acc, w_in, w_all, pgh, pgl, gh, gl, bh, bl, oh, ol,
    sent, got,
):
    row, col = lax.axis_index("row"), lax.axis_index("col")
    bits = n.bit_length() - 1
    row_bit = [(row // (1 << k)) % 2 for k in range(bits)]
    partner = [(row + (1 << k) * (1 - 2 * row_bit[k]), col) for k in range(bits)]
    across = (row, 1 - col)
    slot = sum(row_bit[k] * (1 << (bits - 1 - k)) for k in range(bits))
    order = partner[:2] + [across] + partner[2:]
    order_bit = row_bit[:2] + [col] + row_bit[2:]
    levels = len(order)
    w_slot = sum(order_bit[u] * (1 << (levels - 1 - u)) for u in range(levels))

    barrier = pltpu.get_barrier_semaphore()
    for device in order:
        pl.semaphore_signal(
            barrier, inc=1, device_id=device, device_id_type=pl.DeviceIdType.MESH
        )
    pl.semaphore_wait(barrier, levels)

    used = []

    def send(src, dst, device):
        k = len(used)
        used.append(k)
        copy = pltpu.make_async_remote_copy(
            src_ref=src,
            dst_ref=dst,
            send_sem=sent.at[k],
            recv_sem=got.at[k],
            device_id=device,
            device_id_type=pl.DeviceIdType.MESH,
        )
        copy.start()
        return copy

    def gather(buffer, place, t, device):
        window = pl.ds((place // (1 << t)) * (1 << t), 1 << t)
        return send(buffer.at[window], buffer.at[window], device)

    def scatter(acc, into, place, q, device):
        keep = (place // (1 << q)) * (1 << q)
        away = keep + (1 << q) * (1 - 2 * ((place // (1 << q)) % 2))
        return send(acc.at[pl.ds(away, 1 << q)], into.at[pl.ds(1 << q, 1 << q)], device)

    def add(acc, into, place, q):
        keep = (place // (1 << q)) * (1 << q)

        def one(k, carry):
            acc[keep + k] = acc[keep + k] + into[(1 << q) + k]
            return carry

        lax.fori_loop(0, 1 << q, one, 0)

    def next_right(t):
        return gather(b_raw, slot, t, partner[bits - 1 - t])

    def next_scatter(u):
        return scatter(r_acc, r_in, slot, bits - 1 - u, partner[u])

    def next_weight(u):
        return scatter(w_acc, w_in, w_slot, levels - 1 - u, order[u])

    a_raw[col] = left[...]
    b_raw[slot] = mine[...]
    right_copy = next_right(0)
    left_copy = send(a_raw.at[col], a_raw.at[col], across)

    column_sums = split_grad(pg, pgh, pgl)
    groups = pgh.shape[0] // (2 * tj)
    cut = groups // 4
    make_grad_outer(pgh, pgl, w, gh, gl, tj, 0, cut)
    for t in range(1, bits - 1):
        right_copy.wait()
        right_copy = next_right(t)
        if t == 1:
            make_grad_outer(pgh, pgl, w, gh, gl, tj, cut, groups)
    left_copy.wait()
    a = jnp.concatenate([a_raw[0], a_raw[1]], axis=0)
    make_grad_right(a, gh, gl, r_acc, 4 * tj)
    r_copy = next_scatter(0)
    r_copy.wait()
    add(r_acc, r_in, slot, bits - 1)
    r_copy = next_scatter(1)
    right_copy.wait()
    right_copy = next_right(bits - 1)
    right_copy.wait()

    split_right(b_raw, bh, bl, 4 * tj)
    make_outer(a, bh, bl, oh, ol, tj)
    r_copy.wait()
    add(r_acc, r_in, slot, bits - 2)
    r_copy = next_scatter(2)
    make_grad_weight(oh, ol, pgh, pgl, w_acc, column_sums, scale)
    w_copy = next_weight(0)
    size = gh.shape[0] // 2
    make_grad_left(bh, bl, gh, gl, l_part, 0, size)
    w_copy.wait()
    add(w_acc, w_in, w_slot, levels - 1)
    w_copy = next_weight(1)
    r_copy.wait()
    add(r_acc, r_in, slot, bits - 3)
    for u in range(3, bits):
        r_copy = next_scatter(u)
        if u == 3:
            make_grad_left(bh, bl, gh, gl, l_part, size, 2 * size)
            left_copy = send(l_part.at[1 - col], l_in, across)
        if u < bits - 1:
            r_copy.wait()
            add(r_acc, r_in, slot, bits - 1 - u)
    steps = pgh.shape[0] // (2 * tj)
    parts = 2 * levels - 2
    at = [steps * k // parts for k in range(parts + 1)]

    def some_out(k):
        if at[k] < at[k + 1]:
            make_pair_out(oh, ol, w, bias, out, 2 * tj, at[k], at[k + 1])

    for u in range(1, levels):
        some_out(u - 1)
        w_copy.wait()
        add(w_acc, w_in, w_slot, levels - 1 - u)
        if u < levels - 1:
            w_copy = next_weight(u + 1)
        if u == 2:
            r_copy.wait()
            add(r_acc, r_in, slot, 0)
            grad_right[...] = r_acc[slot]
    piece = w_all.shape[1]
    w_all[w_slot] = w_acc[w_slot, :piece, :]
    grad_bias[...] = jnp.sum(w_acc[w_slot, piece:, :], axis=0, keepdims=True)
    for t in range(levels):
        w_copy = gather(w_all, w_slot, t, order[levels - 1 - t])
        if t < levels - 1:
            some_out(levels - 1 + t)
        else:
            left_copy.wait()
            grad_left[...] = l_part[col] + l_in[...]
        w_copy.wait()
    grad_weight[...] = w_all[...]


def fast(left, right, w_out, b_out, pair_grad):
    ti = left.shape[1] // C
    tj = right.shape[1] // C
    pairs = ti * tj
    n = lax.axis_size("row")
    devices = n * lax.axis_size("col")
    piece = C * C // devices
    bits = n.bit_length() - 1
    copies = 2 * bits + 2 * (bits + 1) + 2
    vmem = pl.BlockSpec(memory_space=pltpu.VMEM)
    w = w_out.reshape(C, C, Z).transpose(1, 0, 2).reshape(C * C, Z)
    mine = right.reshape(-1, tj, C).transpose(0, 2, 1).reshape(right.shape)
    shape = jax.ShapeDtypeStruct
    scratch = [
        ((2,) + left.shape, F32),
        ((n,) + right.shape, F32),
        ((n,) + right.shape, F32),
        ((n,) + right.shape, F32),
        ((2,) + left.shape, F32),
        (left.shape, F32),
        ((devices, piece + 8, Z), F32),
        ((devices, piece + 8, Z), F32),
        ((devices, piece, Z), F32),
        ((pairs, Z), BF),
        ((pairs, Z), BF),
        ((ti * C, C * tj), BF),
        ((ti * C, C * tj), BF),
        ((S, C * tj), BF),
        ((S, C * tj), BF),
        ((C * C, pairs), BF),
        ((C * C, pairs), BF),
    ]
    out, grad_left, grad_right, gw, gb = pl.pallas_call(
        functools.partial(kernel, n, tj, 1.0 / (ti * n)),
        out_shape=[
            shape((pairs, Z), F32),
            shape(left.shape, F32),
            shape(right.shape, F32),
            shape((devices, piece, Z), F32),
            shape((1, Z), F32),
        ],
        in_specs=[vmem] * 5,
        out_specs=[vmem] * 5,
        scratch_shapes=[pltpu.VMEM(*s) for s in scratch]
        + [pltpu.SemaphoreType.DMA((copies,)), pltpu.SemaphoreType.DMA((copies,))],
        compiler_params=pltpu.CompilerParams(
            vmem_limit_bytes=56 * 1024 * 1024, collective_id=0, has_side_effects=True
        ),
        cost_estimate=pl.CostEstimate(
            flops=36 * pairs * C * C * Z, bytes_accessed=1 << 23, transcendentals=0
        ),
        name="outer_product_mean",
    )(left, mine, pair_grad.reshape(pairs, Z), w, b_out.reshape(1, Z))
    grad_weight = gw.reshape(C, C, Z).transpose(1, 0, 2).reshape(C * C, Z)
    grad_right = grad_right.reshape(-1, C, tj).transpose(0, 2, 1).reshape(right.shape)
    return (out.reshape(pair_grad.shape), grad_left, grad_right, grad_weight, gb.reshape(Z))


def plain(left, right, w_out, b_out, pair_grad):
    high = lax.Precision.HIGHEST
    ti = left.shape[1] // C
    tj = right.shape[1] // C
    residues = ti * lax.axis_size("row")
    cube = w_out.reshape(C, C, Z)
    a = lax.all_gather(left, "col", axis=0, tiled=True)
    b = lax.all_gather(right, "row", axis=0, tiled=True)
    outer = lax.dot_general(a, b, (((0,), (0,)), ((), ())), precision=high) / S
    cut = outer.reshape(ti, C, tj, C)
    pair_out = jnp.einsum("icje,cez->ijz", cut, cube, precision=high) + b_out
    g = jnp.einsum("ijz,cez->icje", pair_grad, cube, precision=high)
    g = g.reshape(ti * C, tj * C)
    part = lax.dot_general(b, g, NT, precision=high) / S
    grad_left = lax.psum_scatter(part, "col", scatter_dimension=0, tiled=True)
    part = jnp.dot(a, g, precision=high) / S
    grad_right = lax.psum_scatter(part, "row", scatter_dimension=0, tiled=True)
    gw = jnp.einsum("icje,ijz->cez", cut, pair_grad, precision=high).reshape(C * C, Z)
    gw, gb = lax.psum((gw, jnp.sum(pair_grad, axis=(0, 1))), ("row", "col"))
    return (pair_out, grad_left, grad_right, gw / residues, gb / residues)


def body(left, right, w_out, b_out, pair_grad):
    n, m = lax.axis_size("row"), lax.axis_size("col")
    fits = (
        (right.shape[1] // C) % LANES == 0
        and (left.shape[1] // C) % 8 == 0
        and m == 2
        and n >= 16
        and n & (n - 1) == 0
        and right.shape[0] % 8 == 0
        and (C * C) % (8 * n * m) == 0
    )
    return (fast if fits else plain)(left, right, w_out, b_out, pair_grad)


def solution(mesh):
    placed = (P("col", "row"), P("row", "col"), P(), P(), P("row", "col", None))
    return jax.shard_map(
        body,
        mesh=mesh,
        in_specs=placed,
        out_specs=(P("row", "col", None), P("col", "row"), P("row", "col"), P(), P()),
        check_vma=False,
    )
```

```python
import functools

import jax
import jax.numpy as jnp
from jax import lax
from jax.experimental import pallas as pl
from jax.experimental.pallas import tpu as pltpu
from jax.sharding import PartitionSpec as P

C = 32
Z = 128
S = 128
LANES = 128
BF = jnp.bfloat16
F32 = jnp.float32
NN = (((1,), (0,)), ((), ()))
NT = (((1,), (1,)), ((), ()))


def split(x):
    high = x.astype(BF)
    return high, (x - high.astype(F32)).astype(BF)


def mm(a, b, dims):
    return lax.dot_general(a, b, dims, preferred_element_type=F32)


def bit_reverse(value, bits):
    return sum(((value >> k) & 1) << (bits - 1 - k) for k in range(bits))


def split_grad(pg, pgh, pgl):
    rows = pg.shape[0]
    step = min(rows, 512)

    def one(k, total):
        at = pl.ds(pl.multiple_of(k * step, step), step)
        x = pg[at, :]
        high, low = split(x)
        pgh[at, :] = high
        pgl[at, :] = low
        return total + jnp.sum(x.reshape(step // 8, 8, x.shape[1]), axis=0)

    return lax.fori_loop(0, rows // step, one, jnp.zeros((8, pg.shape[1]), F32))


def make_grad_outer(pgh, pgl, w, gh, gl, tj, first, last):
    wh, wl = split(w[...])
    both = jnp.concatenate([wh, wl], axis=1)
    group = 2

    def one(k, carry):
        at = pl.ds(pl.multiple_of(k * group * tj, group * tj), group * tj)
        ph, low = pgh[at, :], pgl[at, :]
        g = mm(both, jnp.concatenate([ph, ph], axis=1), NT) + mm(wh, low, NT)
        high, low = split(g)
        for i in range(group):
            rows = pl.ds(pl.multiple_of(k * group * C + i * C, C), C)
            for e in range(C):
                gh[rows, e * tj : (e + 1) * tj] = high[e * C : (e + 1) * C, i * tj : (i + 1) * tj]
                gl[rows, e * tj : (e + 1) * tj] = low[e * C : (e + 1) * C, i * tj : (i + 1) * tj]
        return carry

    lax.fori_loop(first, last, one, 0)


def make_grad_right(a, gh, gl, acc, width):
    n, rows, _ = acc.shape
    bits = n.bit_length() - 1
    ah, al = split(a * (1.0 / S))
    both = jnp.concatenate([ah, al], axis=0)

    def one(k, carry):
        cols = pl.ds(pl.multiple_of(k * width, width), width)
        high, low = gh[:, cols], gl[:, cols]
        r = mm(both, high, NN)
        r = r[:S] + r[S:] + mm(ah, low, NN)
        for p in range(n):
            acc[bit_reverse(p, bits), :, cols] = r[p * rows : (p + 1) * rows]
        return carry

    lax.fori_loop(0, gh.shape[1] // width, one, 0)


def split_right(raw, steps, bh, bl, base, width):
    n = raw.shape[0]
    slots = [sum(((p >> k) & 1) << t for t, k in enumerate(steps)) for p in range(n)]

    def one(k, carry):
        cols = pl.ds(pl.multiple_of(k * width, width), width)
        to = pl.ds(pl.multiple_of(base + k * width, width), width)
        high, low = split(jnp.concatenate([raw[slot, :, cols] for slot in slots], axis=0))
        bh[:, to] = high
        bl[:, to] = low
        return carry

    lax.fori_loop(0, raw.shape[2] // width, one, 0)


def make_outer(a, bh, bl, oh, ol, tj):
    ath, atl = split(a.T * (1.0 / S))
    both = jnp.concatenate([ath, atl], axis=1)
    ti = a.shape[1] // C
    group = 4
    width = group * tj

    def one(k, carry):
        cols = pl.ds(pl.multiple_of(k * width, width), width)
        high, low = bh[:, cols], bl[:, cols]
        o = mm(both, jnp.concatenate([high, high], axis=0), NN) + mm(ath, low, NN)
        high, low = split(o)
        for e in range(group):
            rows = pl.ds(pl.multiple_of(k * group * C + e * C, C), C)
            for i in range(ti):
                oh[rows, i * tj : (i + 1) * tj] = high[i * C : (i + 1) * C, e * tj : (e + 1) * tj]
                ol[rows, i * tj : (i + 1) * tj] = low[i * C : (i + 1) * C, e * tj : (e + 1) * tj]
        return carry

    lax.fori_loop(0, bh.shape[1] // width, one, 0)


def make_grad_weight(oh, ol, pgh, pgl, acc, column_sums, scale, half):
    slots, held, _ = acc.shape
    piece = held - 8
    group = 256 // piece
    step = group * piece

    def one(turn, carry):
        k = half * (slots // group // 2) + turn
        rows = pl.ds(pl.multiple_of(k * step, step), step)
        ph = pgh[...]
        r = mm(oh[rows, :], jnp.concatenate([ph, pgl[...]], axis=1), NN)
        r = (r[:, :Z] + r[:, Z:] + mm(ol[rows, :], ph, NN)) * scale
        for g in range(group):
            acc[k * group + g, :piece, :] = r[g * piece : (g + 1) * piece]
            acc[k * group + g, piece:, :] = column_sums * scale
        return carry

    lax.fori_loop(0, slots // group // 2, one, 0)


def make_pair_out(oh, ol, w, bias, out, width, first, last):
    wh, wl = split(w[...].T)
    both = jnp.concatenate([wh, wl], axis=0)

    def one(k, carry):
        cols = pl.ds(pl.multiple_of(k * width, width), width)
        r = mm(both, oh[:, cols], NN)
        r = r[:Z] + r[Z:] + mm(wh, ol[:, cols], NN)
        out[cols, :] = r.T + bias[...]
        return carry

    lax.fori_loop(first, last, one, 0)


def make_grad_left(bh, bl, gh, gl, part, first, last):
    both = jnp.concatenate([bh[...], bl[...]], axis=0)
    r = mm(both, gh[first:last, :], NT)
    r = (r[:S] + r[S:] + mm(bh[...], gl[first:last, :], NT)) * (1.0 / S)
    half = part.shape[1]
    for h in range(2):
        part[h, :, first:last] = r[h * half : (h + 1) * half]


def kernel(
    n, tj, scale, left, mine, pg, w_cube, bias, out, grad_left, grad_right, grad_weight, grad_bias,
    a_raw, b_one, b_two, r_acc, r_in, l_part, l_in, w_acc, w_in, w_all, w, pgh, pgl, gh, gl, bh, bl, oh, ol,
    sent, got,
):
    row, col = lax.axis_index("row"), lax.axis_index("col")
    bits = n.bit_length() - 1
    row_bit = [(row // (1 << k)) % 2 for k in range(bits)]
    partner = [(row + (1 << k) * (1 - 2 * row_bit[k]), col) for k in range(bits)]
    across = (row, 1 - col)
    slot = sum(row_bit[k] * (1 << (bits - 1 - k)) for k in range(bits))
    order = partner[:2] + [across] + partner[2:]
    order_bit = row_bit[:2] + [col] + row_bit[2:]
    levels = len(order)
    w_slot = sum(order_bit[u] * (1 << (levels - 1 - u)) for u in range(levels))
    group = 1 << (levels - 2)
    others = []
    for d in range(1, group):
        other_row, other_col, other_slot = row, col, w_slot
        for u in range(2, levels):
            weight = 1 << (levels - 1 - u)
            if d & weight:
                other_slot = other_slot + weight * (1 - 2 * order_bit[u])
                if u == 2:
                    other_col = 1 - col
                else:
                    other_row = other_row + (1 << (u - 1)) * (1 - 2 * order_bit[u])
        others.append((d, (other_row, other_col), other_slot))
    steps_one = [*range(bits - 1, -1, -1)]
    steps_two = [1, *range(bits - 1, 1, -1), 0]
    slot_two = sum(row_bit[k] * (1 << t) for t, k in enumerate(steps_two))

    barrier = pltpu.get_barrier_semaphore()
    greeted = order[:2] + [device for _, device, _ in others]
    for device in greeted:
        pl.semaphore_signal(
            barrier, inc=1, device_id=device, device_id_type=pl.DeviceIdType.MESH
        )
    pl.semaphore_wait(barrier, len(greeted))

    used = []

    def send(src, dst, device):
        k = len(used)
        used.append(k)
        copy = pltpu.make_async_remote_copy(
            src_ref=src,
            dst_ref=dst,
            send_sem=sent.at[k],
            recv_sem=got.at[k],
            device_id=device,
            device_id_type=pl.DeviceIdType.MESH,
        )
        copy.start()
        return copy

    def gather(buffer, place, t, device):
        window = pl.ds((place // (1 << t)) * (1 << t), 1 << t)
        return send(buffer.at[window], buffer.at[window], device)

    def scatter(acc, into, place, q, device):
        keep = (place // (1 << q)) * (1 << q)
        away = keep + (1 << q) * (1 - 2 * ((place // (1 << q)) % 2))
        return send(acc.at[pl.ds(away, 1 << q)], into.at[pl.ds(1 << q, 1 << q)], device)

    def add(acc, into, place, q):
        keep = (place // (1 << q)) * (1 << q)

        def one(k, carry):
            acc[keep + k] = acc[keep + k] + into[(1 << q) + k]
            return carry

        lax.fori_loop(0, 1 << q, one, 0)

    def next_right(t):
        return (
            gather(b_one, slot, t, partner[steps_one[t]]),
            gather(b_two, slot_two, t, partner[steps_two[t]]),
        )

    def await_right(copies):
        for copy in copies:
            copy.wait()

    def next_scatter(u):
        return scatter(r_acc, r_in, slot, bits - 1 - u, partner[u])

    def next_weight(u):
        return scatter(w_acc, w_in, w_slot, levels - 1 - u, order[u])

    half_cols = b_one.shape[2]
    a_raw[col] = left[...]
    b_one[slot] = mine[:, :half_cols]
    b_two[slot_two] = mine[:, half_cols:]
    right_copy = next_right(0)
    left_copy = send(a_raw.at[col], a_raw.at[col], across)

    for e in range(C):
        w[e * C : (e + 1) * C, :] = w_cube[:, e, :]
    column_sums = split_grad(pg, pgh, pgl)
    groups = pgh.shape[0] // (2 * tj)
    cuts = [groups // 8 + k * (groups - groups // 8) // (bits - 2) for k in range(bits - 1)]
    make_grad_outer(pgh, pgl, w, gh, gl, tj, 0, cuts[0])
    for t in range(1, bits - 1):
        await_right(right_copy)
        right_copy = next_right(t)
        make_grad_outer(pgh, pgl, w, gh, gl, tj, cuts[t - 1], cuts[t])
    left_copy.wait()
    a = jnp.concatenate([a_raw[0], a_raw[1]], axis=0)
    make_grad_right(a, gh, gl, r_acc, 4 * tj)
    r_copy = next_scatter(0)
    await_right(right_copy)
    right_copy = next_right(bits - 1)
    r_copy.wait()
    add(r_acc, r_in, slot, bits - 1)
    r_copy = next_scatter(1)
    await_right(right_copy)

    split_right(b_one, steps_one, bh, bl, 0, 4 * tj)
    split_right(b_two, steps_two, bh, bl, half_cols, 4 * tj)
    make_outer(a, bh, bl, oh, ol, tj)
    r_copy.wait()
    add(r_acc, r_in, slot, bits - 2)
    r_copy = next_scatter(2)
    make_grad_weight(oh, ol, pgh, pgl, w_acc, column_sums, scale, 1 - order_bit[0])
    w_copy = next_weight(0)
    make_grad_weight(oh, ol, pgh, pgl, w_acc, column_sums, scale, order_bit[0])
    w_copy.wait()
    add(w_acc, w_in, w_slot, levels - 1)
    w_copy = next_weight(1)
    for u in range(3, bits):
        r_copy.wait()
        add(r_acc, r_in, slot, bits - u)
        r_copy = next_scatter(u)
    size = gh.shape[0] // 2
    make_grad_left(bh, bl, gh, gl, l_part, 0, size)
    make_grad_left(bh, bl, gh, gl, l_part, size, 2 * size)
    left_copy = send(l_part.at[1 - col], l_in, across)
    w_copy.wait()
    add(w_acc, w_in, w_slot, levels - 2)
    exchanged = [send(w_acc.at[to], w_in.at[d], device) for d, device, to in others]
    at = [groups * k // 8 for k in (0, 3, 5, 8)]
    make_pair_out(oh, ol, w, bias, out, 2 * tj, at[0], at[1])
    for copy in exchanged:
        copy.wait()
    terms = [w_acc[w_slot]] + [w_in[d] for d, _, _ in others]
    while len(terms) > 1:
        terms = [one + two for one, two in zip(terms[::2], terms[1::2])]
    total = terms[0]
    piece = w_all.shape[1]
    w_all[w_slot] = total[:piece]
    spread = [send(w_all.at[w_slot], w_all.at[w_slot], device) for _, device, _ in others]
    grad_bias[...] = jnp.sum(total[piece:], axis=0, keepdims=True)
    make_pair_out(oh, ol, w, bias, out, 2 * tj, at[1], at[2])
    for copy in spread:
        copy.wait()
    w_copy = gather(w_all, w_slot, levels - 2, order[1])
    make_pair_out(oh, ol, w, bias, out, 2 * tj, at[2], at[3])
    w_copy.wait()
    w_copy = gather(w_all, w_slot, levels - 1, order[0])
    r_copy.wait()
    add(r_acc, r_in, slot, 0)
    grad_right[...] = r_acc[slot]
    left_copy.wait()
    grad_left[...] = l_part[col] + l_in[...]
    w_copy.wait()
    m = C // piece
    for e in range(C):
        grad_weight[:, e, :] = w_all[e * m : (e + 1) * m].reshape(C, w_all.shape[2])


def fast(left, right, w_out, b_out, pair_grad):
    ti = left.shape[1] // C
    tj = right.shape[1] // C
    pairs = ti * tj
    n = lax.axis_size("row")
    devices = n * lax.axis_size("col")
    piece = C * C // devices
    bits = n.bit_length() - 1
    copies = 3 * bits + 6 + 2 * (n // 2 - 1)
    vmem = pl.BlockSpec(memory_space=pltpu.VMEM)
    half = (n, right.shape[0], right.shape[1] // 2)
    mine = right.reshape(-1, tj, C).transpose(0, 2, 1).reshape(right.shape)
    shape = jax.ShapeDtypeStruct
    scratch = [
        ((2,) + left.shape, F32),
        (half, F32),
        (half, F32),
        ((n,) + right.shape, F32),
        ((n,) + right.shape, F32),
        ((2,) + left.shape, F32),
        (left.shape, F32),
        ((devices, piece + 8, Z), F32),
        ((devices, piece + 8, Z), F32),
        ((devices, piece, Z), F32),
        ((C * C, Z), F32),
        ((pairs, Z), BF),
        ((pairs, Z), BF),
        ((ti * C, C * tj), BF),
        ((ti * C, C * tj), BF),
        ((S, C * tj), BF),
        ((S, C * tj), BF),
        ((C * C, pairs), BF),
        ((C * C, pairs), BF),
    ]
    out, grad_left, grad_right, gw, gb = pl.pallas_call(
        functools.partial(kernel, n, tj, 1.0 / (ti * n)),
        out_shape=[
            shape((pairs, Z), F32),
            shape(left.shape, F32),
            shape(right.shape, F32),
            shape((C, C, Z), F32),
            shape((1, Z), F32),
        ],
        in_specs=[vmem] * 5,
        out_specs=[vmem] * 5,
        scratch_shapes=[pltpu.VMEM(*s) for s in scratch]
        + [pltpu.SemaphoreType.DMA((copies,)), pltpu.SemaphoreType.DMA((copies,))],
        compiler_params=pltpu.CompilerParams(
            vmem_limit_bytes=56 * 1024 * 1024, collective_id=0, has_side_effects=True
        ),
        cost_estimate=pl.CostEstimate(
            flops=36 * pairs * C * C * Z, bytes_accessed=1 << 23, transcendentals=0
        ),
        name="outer_product_mean",
    )(left, mine, pair_grad.reshape(pairs, Z), w_out.reshape(C, C, Z), b_out.reshape(1, Z))
    grad_weight = gw.reshape(C * C, Z)
    grad_right = grad_right.reshape(-1, C, tj).transpose(0, 2, 1).reshape(right.shape)
    return (out.reshape(pair_grad.shape), grad_left, grad_right, grad_weight, gb.reshape(Z))


def plain(left, right, w_out, b_out, pair_grad):
    high = lax.Precision.HIGHEST
    ti = left.shape[1] // C
    tj = right.shape[1] // C
    residues = ti * lax.axis_size("row")
    cube = w_out.reshape(C, C, Z)
    a = lax.all_gather(left, "col", axis=0, tiled=True)
    b = lax.all_gather(right, "row", axis=0, tiled=True)
    outer = lax.dot_general(a, b, (((0,), (0,)), ((), ())), precision=high) / S
    cut = outer.reshape(ti, C, tj, C)
    pair_out = jnp.einsum("icje,cez->ijz", cut, cube, precision=high) + b_out
    g = jnp.einsum("ijz,cez->icje", pair_grad, cube, precision=high)
    g = g.reshape(ti * C, tj * C)
    part = lax.dot_general(b, g, NT, precision=high) / S
    grad_left = lax.psum_scatter(part, "col", scatter_dimension=0, tiled=True)
    part = jnp.dot(a, g, precision=high) / S
    grad_right = lax.psum_scatter(part, "row", scatter_dimension=0, tiled=True)
    gw = jnp.einsum("icje,ijz->cez", cut, pair_grad, precision=high).reshape(C * C, Z)
    gw, gb = lax.psum((gw, jnp.sum(pair_grad, axis=(0, 1))), ("row", "col"))
    return (pair_out, grad_left, grad_right, gw / residues, gb / residues)


def body(left, right, w_out, b_out, pair_grad):
    n, m = lax.axis_size("row"), lax.axis_size("col")
    fits = (
        (right.shape[1] // C) % LANES == 0
        and (left.shape[1] // C) % 8 == 0
        and m == 2
        and n >= 16
        and n & (n - 1) == 0
        and right.shape[0] % 8 == 0
        and (C * C) % (8 * n * m) == 0
    )
    return (fast if fits else plain)(left, right, w_out, b_out, pair_grad)


def solution(mesh):
    placed = (P("col", "row"), P("row", "col"), P(), P(), P("row", "col", None))
    return jax.shard_map(
        body,
        mesh=mesh,
        in_specs=placed,
        out_specs=(P("row", "col", None), P("col", "row"), P("row", "col"), P(), P()),
        check_vma=False,
    )
```

```python
import functools

import jax
import jax.numpy as jnp
from jax import lax
from jax.experimental import pallas as pl
from jax.experimental.pallas import tpu as pltpu
from jax.sharding import PartitionSpec as P

C = 32
Z = 128
S = 128
LANES = 128
BF = jnp.bfloat16
F32 = jnp.float32
NN = (((1,), (0,)), ((), ()))
NT = (((1,), (1,)), ((), ()))


def split(x):
    high = x.astype(BF)
    return high, (x - high.astype(F32)).astype(BF)


def mm(a, b, dims):
    return lax.dot_general(a, b, dims, preferred_element_type=F32)


def bit_reverse(value, bits):
    return sum(((value >> k) & 1) << (bits - 1 - k) for k in range(bits))


def split_grad(pg, pgh, pgl):
    rows = pg.shape[0]
    step = min(rows, 512)

    def one(k, total):
        at = pl.ds(pl.multiple_of(k * step, step), step)
        x = pg[at, :]
        high, low = split(x)
        pgh[at, :] = high
        pgl[at, :] = low
        return total + jnp.sum(x.reshape(step // 8, 8, x.shape[1]), axis=0)

    return lax.fori_loop(0, rows // step, one, jnp.zeros((8, pg.shape[1]), F32))


def make_grad_outer(pgh, pgl, w, gh, gl, tj, first, last):
    wh, wl = split(w[...])
    both = jnp.concatenate([wh, wl], axis=1)
    group = 2

    def one(k, carry):
        at = pl.ds(pl.multiple_of(k * group * tj, group * tj), group * tj)
        ph, low = pgh[at, :], pgl[at, :]
        g = mm(both, jnp.concatenate([ph, ph], axis=1), NT) + mm(wh, low, NT)
        high, low = split(g)
        for i in range(group):
            rows = pl.ds(pl.multiple_of(k * group * C + i * C, C), C)
            for e in range(C):
                gh[rows, e * tj : (e + 1) * tj] = high[e * C : (e + 1) * C, i * tj : (i + 1) * tj]
                gl[rows, e * tj : (e + 1) * tj] = low[e * C : (e + 1) * C, i * tj : (i + 1) * tj]
        return carry

    lax.fori_loop(first, last, one, 0)


def make_grad_right(a, gh, gl, acc, width):
    n, rows, _ = acc.shape
    bits = n.bit_length() - 1
    ah, al = split(a * (1.0 / S))
    both = jnp.concatenate([ah, al], axis=0)

    def one(k, carry):
        cols = pl.ds(pl.multiple_of(k * width, width), width)
        high, low = gh[:, cols], gl[:, cols]
        r = mm(both, high, NN)
        r = r[:S] + r[S:] + mm(ah, low, NN)
        for p in range(n):
            acc[bit_reverse(p, bits), :, cols] = r[p * rows : (p + 1) * rows]
        return carry

    lax.fori_loop(0, gh.shape[1] // width, one, 0)


def split_right(raw, steps, bh, bl, base, width):
    n = raw.shape[0]
    slots = [sum(((p >> k) & 1) << t for t, k in enumerate(steps)) for p in range(n)]

    def one(k, carry):
        cols = pl.ds(pl.multiple_of(k * width, width), width)
        to = pl.ds(pl.multiple_of(base + k * width, width), width)
        high, low = split(jnp.concatenate([raw[slot, :, cols] for slot in slots], axis=0))
        bh[:, to] = high
        bl[:, to] = low
        return carry

    lax.fori_loop(0, raw.shape[2] // width, one, 0)


def make_outer(a, bh, bl, oh, ol, tj):
    ath, atl = split(a.T * (1.0 / S))
    both = jnp.concatenate([ath, atl], axis=1)
    ti = a.shape[1] // C
    group = 4
    width = group * tj

    def one(k, carry):
        cols = pl.ds(pl.multiple_of(k * width, width), width)
        high, low = bh[:, cols], bl[:, cols]
        o = mm(both, jnp.concatenate([high, high], axis=0), NN) + mm(ath, low, NN)
        high, low = split(o)
        for e in range(group):
            rows = pl.ds(pl.multiple_of(k * group * C + e * C, C), C)
            for i in range(ti):
                oh[rows, i * tj : (i + 1) * tj] = high[i * C : (i + 1) * C, e * tj : (e + 1) * tj]
                ol[rows, i * tj : (i + 1) * tj] = low[i * C : (i + 1) * C, e * tj : (e + 1) * tj]
        return carry

    lax.fori_loop(0, bh.shape[1] // width, one, 0)


def make_grad_weight(oh, ol, pgh, pgl, acc, column_sums, scale, quarter, count=1):
    slots, held, _ = acc.shape
    piece = held - 8
    group = min(256 // piece, slots // 4)
    step = group * piece

    def one(turn, carry):
        k = quarter * (slots // group // 4) + turn
        rows = pl.ds(pl.multiple_of(k * step, step), step)
        ph = pgh[...]
        r = mm(oh[rows, :], jnp.concatenate([ph, pgl[...]], axis=1), NN)
        r = (r[:, :Z] + r[:, Z:] + mm(ol[rows, :], ph, NN)) * scale
        for g in range(group):
            acc[k * group + g, :piece, :] = r[g * piece : (g + 1) * piece]
            acc[k * group + g, piece:, :] = column_sums * scale
        return carry

    lax.fori_loop(0, slots // group // 4 * count, one, 0)


def make_pair_out(oh, ol, w, bias, out, width, first, last):
    wh, wl = split(w[...].T)
    both = jnp.concatenate([wh, wl], axis=0)

    def one(k, carry):
        cols = pl.ds(pl.multiple_of(k * width, width), width)
        r = mm(both, oh[:, cols], NN)
        r = r[:Z] + r[Z:] + mm(wh, ol[:, cols], NN)
        out[cols, :] = r.T + bias[...]
        return carry

    lax.fori_loop(first, last, one, 0)


def make_grad_left(bh, bl, gh, gl, part, first, last):
    both = jnp.concatenate([bh[...], bl[...]], axis=0)
    r = mm(both, gh[first:last, :], NT)
    r = (r[:S] + r[S:] + mm(bh[...], gl[first:last, :], NT)) * (1.0 / S)
    half = part.shape[1]
    for h in range(2):
        part[h, :, first:last] = r[h * half : (h + 1) * half]


def kernel(
    n, tj, scale, left, mine, pg, w_cube, bias, out, grad_left, grad_right, grad_weight, grad_bias,
    a_raw, b_one, b_two, r_acc, r_in, l_part, l_in, w_acc, w_in, w_all, w, pgh, pgl, gh, gl, bh, bl, oh, ol,
    sent, got,
):
    row, col = lax.axis_index("row"), lax.axis_index("col")
    bits = n.bit_length() - 1
    row_bit = [(row // (1 << k)) % 2 for k in range(bits)]
    partner = [(row + (1 << k) * (1 - 2 * row_bit[k]), col) for k in range(bits)]
    across = (row, 1 - col)
    slot = sum(row_bit[k] * (1 << (bits - 1 - k)) for k in range(bits))
    order = partner[:2] + [across] + partner[2:]
    order_bit = row_bit[:2] + [col] + row_bit[2:]
    levels = len(order)
    w_slot = sum(order_bit[u] * (1 << (levels - 1 - u)) for u in range(levels))
    group = 1 << (levels - 2)
    others = []
    for d in range(1, group):
        other_row, other_col, other_slot = row, col, w_slot
        for u in range(2, levels):
            weight = 1 << (levels - 1 - u)
            if d & weight:
                other_slot = other_slot + weight * (1 - 2 * order_bit[u])
                if u == 2:
                    other_col = 1 - col
                else:
                    other_row = other_row + (1 << (u - 1)) * (1 - 2 * order_bit[u])
        others.append((d, (other_row, other_col), other_slot))
    steps_one = [*range(bits - 1, -1, -1)]
    steps_two = [1, *range(bits - 1, 1, -1), 0]
    slot_two = sum(row_bit[k] * (1 << t) for t, k in enumerate(steps_two))

    barrier = pltpu.get_barrier_semaphore()
    greeted = order[:2] + [device for _, device, _ in others]
    for device in greeted:
        pl.semaphore_signal(
            barrier, inc=1, device_id=device, device_id_type=pl.DeviceIdType.MESH
        )
    pl.semaphore_wait(barrier, len(greeted))

    used = []

    def send(src, dst, device):
        k = len(used)
        used.append(k)
        copy = pltpu.make_async_remote_copy(
            src_ref=src,
            dst_ref=dst,
            send_sem=sent.at[k],
            recv_sem=got.at[k],
            device_id=device,
            device_id_type=pl.DeviceIdType.MESH,
        )
        copy.start()
        return copy

    def gather(buffer, place, t, device):
        window = pl.ds((place // (1 << t)) * (1 << t), 1 << t)
        return send(buffer.at[window], buffer.at[window], device)

    def scatter(acc, into, place, q, device):
        keep = (place // (1 << q)) * (1 << q)
        away = keep + (1 << q) * (1 - 2 * ((place // (1 << q)) % 2))
        return send(acc.at[pl.ds(away, 1 << q)], into.at[pl.ds(1 << q, 1 << q)], device)

    def add(acc, into, place, q):
        keep = (place // (1 << q)) * (1 << q)

        def one(k, carry):
            acc[keep + k] = acc[keep + k] + into[(1 << q) + k]
            return carry

        lax.fori_loop(0, 1 << q, one, 0)

    def add_weight(quarter):
        size = 1 << (levels - 2)
        start = quarter * size
        came = (1 << (levels - 1)) + (quarter % 2) * size

        def one(k, carry):
            w_acc[start + k] = w_acc[start + k] + w_in[came + k]
            return carry

        lax.fori_loop(0, size, one, 0)

    def next_right(t):
        return (
            gather(b_one, slot, t, partner[steps_one[t]]),
            gather(b_two, slot_two, t, partner[steps_two[t]]),
        )

    def await_right(copies):
        for copy in copies:
            copy.wait()

    def next_scatter(u):
        return scatter(r_acc, r_in, slot, bits - 1 - u, partner[u])

    def next_weight(u):
        return scatter(w_acc, w_in, w_slot, levels - 1 - u, order[u])

    half_cols = b_one.shape[2]
    a_raw[col] = left[...]
    b_one[slot] = mine[:, :half_cols]
    b_two[slot_two] = mine[:, half_cols:]
    right_copy = next_right(0)
    left_copy = send(a_raw.at[col], a_raw.at[col], across)

    for e in range(C):
        w[e * C : (e + 1) * C, :] = w_cube[:, e, :]
    column_sums = split_grad(pg, pgh, pgl)
    groups = pgh.shape[0] // (2 * tj)
    cuts = [min(groups, groups // 8 + k * 5 * groups // 8) for k in range(bits - 2)] + [groups]
    make_grad_outer(pgh, pgl, w, gh, gl, tj, 0, cuts[0])
    for t in range(1, bits - 1):
        await_right(right_copy)
        right_copy = next_right(t)
        make_grad_outer(pgh, pgl, w, gh, gl, tj, cuts[t - 1], cuts[t])
    left_copy.wait()
    a = jnp.concatenate([a_raw[0], a_raw[1]], axis=0)
    make_grad_right(a, gh, gl, r_acc, 4 * tj)
    r_copy = next_scatter(0)
    await_right(right_copy)
    right_copy = next_right(bits - 1)
    r_copy.wait()
    add(r_acc, r_in, slot, bits - 1)
    r_copy = next_scatter(1)
    right_copy[0].wait()
    split_right(b_one, steps_one, bh, bl, 0, 4 * tj)
    right_copy[1].wait()
    split_right(b_two, steps_two, bh, bl, half_cols, 4 * tj)
    make_outer(a, bh, bl, oh, ol, tj)
    r_copy.wait()
    add(r_acc, r_in, slot, bits - 2)
    r_copy = next_scatter(2)
    weight = functools.partial(make_grad_weight, oh, ol, pgh, pgl, w_acc, column_sums, scale)
    mine_first, mine_last = 2 * order_bit[0] + 1 - order_bit[1], 2 * order_bit[0] + order_bit[1]
    weight(2 - 2 * order_bit[0], 2)
    w_copy = next_weight(0)
    weight(mine_first)
    w_copy.wait()
    add_weight(mine_first)
    w_copy = next_weight(1)
    weight(mine_last)
    add_weight(mine_last)
    for u in range(3, bits):
        r_copy.wait()
        add(r_acc, r_in, slot, bits - u)
        r_copy = next_scatter(u)
    size = gh.shape[0] // 2
    make_grad_left(bh, bl, gh, gl, l_part, 0, size)
    w_copy.wait()
    add(w_acc, w_in, w_slot, levels - 2)
    exchanged = [send(w_acc.at[to], w_in.at[d], device) for d, device, to in others]
    make_grad_left(bh, bl, gh, gl, l_part, size, 2 * size)
    left_copy = send(l_part.at[1 - col], l_in, across)
    at = [groups * k // 8 for k in (0, 1, 4, 7, 8)]
    make_pair_out(oh, ol, w, bias, out, 2 * tj, at[0], at[1])
    for copy in exchanged:
        copy.wait()
    terms = [w_acc[w_slot]] + [w_in[d] for d, _, _ in others]
    while len(terms) > 1:
        terms = [one + two for one, two in zip(terms[::2], terms[1::2])]
    total = terms[0]
    piece = w_all.shape[1]
    w_all[w_slot] = total[:piece]
    spread = [send(w_all.at[w_slot], w_all.at[w_slot], device) for _, device, _ in others]
    grad_bias[...] = jnp.sum(total[piece:], axis=0, keepdims=True)
    make_pair_out(oh, ol, w, bias, out, 2 * tj, at[1], at[2])
    for copy in spread:
        copy.wait()
    w_copy = gather(w_all, w_slot, levels - 2, order[1])
    make_pair_out(oh, ol, w, bias, out, 2 * tj, at[2], at[3])
    w_copy.wait()
    w_copy = gather(w_all, w_slot, levels - 1, order[0])
    make_pair_out(oh, ol, w, bias, out, 2 * tj, at[3], at[4])
    r_copy.wait()
    add(r_acc, r_in, slot, 0)
    grad_right[...] = r_acc[slot]
    left_copy.wait()
    grad_left[...] = l_part[col] + l_in[...]
    w_copy.wait()
    m = C // piece
    for e in range(C):
        grad_weight[:, e, :] = w_all[e * m : (e + 1) * m].reshape(C, w_all.shape[2])


def fast(left, right, w_out, b_out, pair_grad):
    ti = left.shape[1] // C
    tj = right.shape[1] // C
    pairs = ti * tj
    n = lax.axis_size("row")
    devices = n * lax.axis_size("col")
    piece = C * C // devices
    bits = n.bit_length() - 1
    copies = 3 * bits + 6 + 2 * (n // 2 - 1)
    vmem = pl.BlockSpec(memory_space=pltpu.VMEM)
    half = (n, right.shape[0], right.shape[1] // 2)
    mine = right.reshape(-1, tj, C).transpose(0, 2, 1).reshape(right.shape)
    shape = jax.ShapeDtypeStruct
    scratch = [
        ((2,) + left.shape, F32),
        (half, F32),
        (half, F32),
        ((n,) + right.shape, F32),
        ((n,) + right.shape, F32),
        ((2,) + left.shape, F32),
        (left.shape, F32),
        ((devices, piece + 8, Z), F32),
        ((devices, piece + 8, Z), F32),
        ((devices, piece, Z), F32),
        ((C * C, Z), F32),
        ((pairs, Z), BF),
        ((pairs, Z), BF),
        ((ti * C, C * tj), BF),
        ((ti * C, C * tj), BF),
        ((S, C * tj), BF),
        ((S, C * tj), BF),
        ((C * C, pairs), BF),
        ((C * C, pairs), BF),
    ]
    out, grad_left, grad_right, gw, gb = pl.pallas_call(
        functools.partial(kernel, n, tj, 1.0 / (ti * n)),
        out_shape=[
            shape((pairs, Z), F32),
            shape(left.shape, F32),
            shape(right.shape, F32),
            shape((C, C, Z), F32),
            shape((1, Z), F32),
        ],
        in_specs=[vmem] * 5,
        out_specs=[vmem] * 5,
        scratch_shapes=[pltpu.VMEM(*s) for s in scratch]
        + [pltpu.SemaphoreType.DMA((copies,)), pltpu.SemaphoreType.DMA((copies,))],
        compiler_params=pltpu.CompilerParams(
            vmem_limit_bytes=56 * 1024 * 1024, collective_id=0, has_side_effects=True
        ),
        cost_estimate=pl.CostEstimate(
            flops=36 * pairs * C * C * Z, bytes_accessed=1 << 23, transcendentals=0
        ),
        name="outer_product_mean",
    )(left, mine, pair_grad.reshape(pairs, Z), w_out.reshape(C, C, Z), b_out.reshape(1, Z))
    grad_weight = gw.reshape(C * C, Z)
    grad_right = grad_right.reshape(-1, C, tj).transpose(0, 2, 1).reshape(right.shape)
    return (out.reshape(pair_grad.shape), grad_left, grad_right, grad_weight, gb.reshape(Z))


def plain(left, right, w_out, b_out, pair_grad):
    high = lax.Precision.HIGHEST
    ti = left.shape[1] // C
    tj = right.shape[1] // C
    residues = ti * lax.axis_size("row")
    cube = w_out.reshape(C, C, Z)
    a = lax.all_gather(left, "col", axis=0, tiled=True)
    b = lax.all_gather(right, "row", axis=0, tiled=True)
    outer = lax.dot_general(a, b, (((0,), (0,)), ((), ())), precision=high) / S
    cut = outer.reshape(ti, C, tj, C)
    pair_out = jnp.einsum("icje,cez->ijz", cut, cube, precision=high) + b_out
    g = jnp.einsum("ijz,cez->icje", pair_grad, cube, precision=high)
    g = g.reshape(ti * C, tj * C)
    part = lax.dot_general(b, g, NT, precision=high) / S
    grad_left = lax.psum_scatter(part, "col", scatter_dimension=0, tiled=True)
    part = jnp.dot(a, g, precision=high) / S
    grad_right = lax.psum_scatter(part, "row", scatter_dimension=0, tiled=True)
    gw = jnp.einsum("icje,ijz->cez", cut, pair_grad, precision=high).reshape(C * C, Z)
    gw, gb = lax.psum((gw, jnp.sum(pair_grad, axis=(0, 1))), ("row", "col"))
    return (pair_out, grad_left, grad_right, gw / residues, gb / residues)


def body(left, right, w_out, b_out, pair_grad):
    n, m = lax.axis_size("row"), lax.axis_size("col")
    fits = (
        (right.shape[1] // C) % LANES == 0
        and (left.shape[1] // C) % 8 == 0
        and m == 2
        and n >= 16
        and n & (n - 1) == 0
        and right.shape[0] % 8 == 0
        and (C * C) % (8 * n * m) == 0
    )
    return (fast if fits else plain)(left, right, w_out, b_out, pair_grad)


def solution(mesh):
    placed = (P("col", "row"), P("row", "col"), P(), P(), P("row", "col", None))
    return jax.shard_map(
        body,
        mesh=mesh,
        in_specs=placed,
        out_specs=(P("row", "col", None), P("col", "row"), P("row", "col"), P(), P()),
        check_vma=False,
    )
```
